32 devices in a mesh: dp: 16 (over z, y, core), tensor: 2 (over x).
Axes of the slice: x: 2, y: 2, z: 4, core: 2. Of those that a mesh axis runs over, the one named last changes fastest.
Arguments:
- tokens: bfloat16 [24000, 512], P(('dp', 'tensor')), may hold values from -16 to 16
- ff_in: bfloat16 [1, 2, 512, 2048], P(None, None, None, ('dp', 'tensor')), may hold values from -0.25 to 0.25
- ff_out: bfloat16 [1, 2, 2048, 512], P(None, None, ('dp', 'tensor')), may hold values from -0.25 to 0.25
- att_qkv: bfloat16 [1, 512, 3, 512], P(None, 'dp', None, 'tensor'), may hold values from -0.25 to 0.25
- att_pos: bfloat16 [1, 512, 512], P(None, 'dp', 'tensor'), may hold values from -0.25 to 0.25
- att_bias: bfloat16 [1, 8, 128], P(None, 'tensor', 'dp'), may hold values from -3 to 3
- att_out: bfloat16 [1, 512, 512], P(None, 'tensor', 'dp'), may hold values from -1 to 1
- conv_in: bfloat16 [1, 512, 2, 512], P(None, None, None, ('dp', 'tensor')), may hold values from -0.25 to 0.25
- conv_depth: bfloat16 [1, 31, 512], P(None, None, ('dp', 'tensor')), may hold values from -1 to 1
- conv_out: bfloat16 [1, 512, 512], P(None, ('dp', 'tensor')), may hold values from -0.25 to 0.25
- gains: float32 [1, 7, 512], P(None, None, ('dp', 'tensor')), may hold values from 0.1 to 1.9
- out_grad: float32 [24000, 512], P(('dp', 'tensor')), may hold values from -6 to 6
Outputs:
- block_out: float32 [24000, 512], P(('dp', 'tensor'))
- tokens_grad: float32 [24000, 512], P(('dp', 'tensor'))
- ff_in_grad: float32 [1, 2, 512, 2048], P(None, None, None, ('dp', 'tensor'))
- ff_out_grad: float32 [1, 2, 2048, 512], P(None, None, ('dp', 'tensor'))
- att_qkv_grad: float32 [1, 512, 3, 512], P(None, 'dp', None, 'tensor')
- att_pos_grad: float32 [1, 512, 512], P(None, 'dp', 'tensor')
- att_bias_grad: float32 [1, 8, 128], P(None, 'tensor', 'dp')
- att_out_grad: float32 [1, 512, 512], P(None, 'tensor', 'dp')
- conv_in_grad: float32 [1, 512, 2, 512], P(None, None, None, ('dp', 'tensor'))
- conv_depth_grad: float32 [1, 31, 512], P(None, None, ('dp', 'tensor'))
- conv_out_grad: float32 [1, 512, 512], P(None, ('dp', 'tensor'))
- gains_grad: float32 [1, 7, 512], P(None, None, ('dp', 'tensor'))
The draws below stay inside these ranges and needn't reach their ends.
All inputs are finite; a program needn't handle non-finite values.
Results may differ from the reference program's by a relative error of at most 0.028.
Values may be sent and summed in bfloat16 or wider, within the bound.
A program may use at most 256 MiB of HBM per device.

```python
import math
import jax
import jax.numpy as jnp
from jax import lax

D = 512
HEADS = 8
FF = 2048
DH = 64
K = 31
LEN = 750
LAYERS = 1
TOKENS = 24000


def draw_tokens(key, part):
    key = jax.random.fold_in(key, 11)
    base_key, common_key = jax.random.split(key)
    seq_total = TOKENS // LEN
    common = jnp.clip(jax.random.normal(common_key, (seq_total, D), jnp.float32), -6.0, 6.0)
    ladder = jnp.arange(seq_total).astype(jnp.float32) / max(seq_total - 1, 1)
    base = jnp.clip(jax.random.normal(base_key, (TOKENS, D), jnp.float32), -6.0, 6.0)
    amplitude = 0.4 + 1.2 * ladder
    offsets = jnp.repeat(common * amplitude[:, None], LEN, axis=0)
    return (base + offsets).astype(jnp.bfloat16)


def steps_of(rng, dims, shards, smallest, high):
    loudness, own = 1.0, jax.random.fold_in(rng, 6)
    for position, shards_of in shards:
        heights = jnp.exp(jax.random.uniform(jax.random.fold_in(own, position), (shards_of,), jnp.float32, smallest / len(shards), high / len(shards)))
        loudness = loudness * jnp.repeat(heights, dims[position] // shards_of).reshape([-1 if axis == position else 1 for axis in range(len(dims))])
    return loudness


def normal_values(own_key, extent, deviation, limit, cuts=(), kind=jnp.bfloat16):
    level = steps_of(own_key, extent, cuts, -0.22, 0.18) if cuts else 1.0
    entries = jax.random.normal(own_key, extent, jnp.float32) * deviation * level
    return jnp.minimum(jnp.maximum(entries, -limit), limit).astype(kind)


def setup_inputs(seed: int = 0) -> dict:
    keys = jax.random.split(jax.random.key(seed), 13)
    return {
        "tokens": draw_tokens(jax.random.fold_in(keys[12], 71), 0),
        "ff_in": normal_values(keys[1], (LAYERS, 2, D, FF), D ** -0.5, 0.25, ((3, 32),)),
        "ff_out": normal_values(keys[2], (LAYERS, 2, FF, D), (FF // 4) ** -0.5, 0.25, ((2, 32),)),
        "att_qkv": normal_values(keys[3], (LAYERS, D, 3, D), D ** -0.5, 0.25, ((1, 16), (3, 2))),
        "att_pos": normal_values(keys[4], (LAYERS, D, D), D ** -0.5, 0.25, ((1, 16), (2, 2))),
        "att_bias": normal_values(keys[5], (LAYERS, HEADS, 2 * DH), 0.5, 3.0, ((1, 2), (2, 16))),
        "att_out": normal_values(keys[6], (LAYERS, D, D), (D // 16) ** -0.5, 1.0, ((1, 2), (2, 16))),
        "conv_in": normal_values(keys[7], (LAYERS, D, 2, D), D ** -0.5, 0.25, ((3, 32),)),
        "conv_depth": normal_values(keys[8], (LAYERS, K, D), K ** -0.5, 1.0, ((2, 32),)),
        "conv_out": normal_values(keys[9], (LAYERS, D, D), D ** -0.5, 0.25, ((1, 32),)),
        "gains": jnp.clip(1.0 + 0.18 * jax.random.normal(keys[10], (LAYERS, 7, D), jnp.float32), 0.1, 1.9),
        "out_grad": normal_values(keys[11], (TOKENS, D), 1.0, 6.0, ((0, 32),), jnp.float32),
    }


EPS = 1e-05
HIGH = lax.Precision.HIGHEST

@jax.custom_vjp
def low(v):
    return lax.optimization_barrier(v.astype(jnp.bfloat16)).astype(jnp.float32)

@jax.custom_vjp
def low_back(v):
    return v

def low_keep(v):
    return (low(v), None)

def low_pass(kept, grad):
    return (grad,)

def back_keep(v):
    return (v, None)

def back_low(kept, grad):
    return (low(grad),)
low.defvjp(low_keep, low_pass)
low_back.defvjp(back_keep, back_low)

def matmul(left, right):
    return jnp.dot(left, right, precision=HIGH, preferred_element_type=jnp.float32)

def layer_norm(inputs, norm_gain):
    centre = inputs - lax.optimization_barrier(jnp.mean(inputs, axis=-1, keepdims=True))
    spread = lax.optimization_barrier(jnp.mean(centre * centre, axis=-1, keepdims=True))
    return centre * lax.rsqrt(spread + EPS) * norm_gain

def position_table(length, model_width):
    distance = (length - 1 - jnp.arange(2 * length - 1)).astype(jnp.float32)
    frequency = jnp.exp(jnp.arange(model_width // 2).astype(jnp.float32) * (-2.0 * math.log(10000.0) / model_width))
    angles = distance[:, None] * frequency[None, :]
    return jnp.stack([jnp.sin(angles), jnp.cos(angles)], axis=-1).reshape(2 * length - 1, model_width)

def rel_shift(matrix):
    head_count, length, span_width = matrix.shape
    padded = jnp.pad(matrix, ((0, 0), (0, 0), (0, 1)))
    flattened = padded.reshape(head_count, length * (span_width + 1))
    flattened = flattened[:, length - 1:length - 1 + length * span_width]
    return flattened.reshape(head_count, length, span_width)[:, :, :length]

def depthwise(signal, kernel):
    tap_count = kernel.shape[0]
    margin = (tap_count - 1) // 2
    length = signal.shape[1]
    padded = jnp.pad(signal, ((0, 0), (margin, tap_count - 1 - margin), (0, 0)))
    summed = jnp.zeros_like(signal)
    for offset in range(tap_count):
        summed = summed + padded[:, offset:offset + length, :] * kernel[offset]
    return summed

def glu_depth(gate_pair, kernel, seq_count):
    gated = gate_pair[:, 0] * jax.nn.sigmoid(gate_pair[:, 1])
    shaped = gated.reshape(seq_count, -1, gated.shape[-1])
    return depthwise(shaped, kernel).reshape(gated.shape)

def feed_forward(residual, w_in, w_out, norm_gain):
    normed = low(layer_norm(residual, norm_gain))
    hidden_pre = low_back(matmul(normed, w_in))
    hidden = low(jax.nn.silu(hidden_pre))
    return residual + 0.5 * low_back(matmul(hidden, w_out))

def attention(residual, w_qkv, w_pos, pos_bias, w_out, norm_gain):
    row_count = residual.shape[0]
    normed = low(layer_norm(residual, norm_gain))
    packed = matmul(normed, w_qkv.reshape(D, 3 * D)).reshape(row_count, 3, HEADS, DH)
    query_rows = low_back(packed[:, 0])
    key_rows = low(low_back(packed[:, 1]))
    value_rows = low(low_back(packed[:, 2]))
    query_a = low(query_rows + pos_bias[:, :DH])
    query_b = low(query_rows + pos_bias[:, DH:])
    pos_table = low(position_table(LEN, D))
    pos_keys = low(low_back(matmul(pos_table, w_pos))).reshape(2 * LEN - 1, HEADS, DH)

    def one_seq(seq_items):
        qa_seq, qb_seq, key_seq, value_seq = seq_items
        content = low_back(jnp.einsum('ihd,jhd->hij', qa_seq, key_seq, precision=HIGH))
        positional = low_back(jnp.einsum('ihd,khd->hik', qb_seq, pos_keys, precision=HIGH))
        scores = (content + rel_shift(positional)) * DH ** (-0.5)
        attn_probs = low(jax.nn.softmax(scores, axis=-1))
        return jnp.einsum('hij,jhd->ihd', attn_probs, value_seq, precision=HIGH)

    def seq_view(array):
        return array.reshape(-1, LEN, HEADS, DH)
    attended = lax.map(jax.checkpoint(one_seq), (seq_view(query_a), seq_view(query_b), seq_view(key_rows), seq_view(value_rows)))
    attended = low(low_back(attended.reshape(row_count, D)))
    return residual + low_back(matmul(attended, w_out))

def convolution(residual, w_in, kernel, w_out, norm_gain, scale_vec, shift_vec):
    row_count = residual.shape[0]
    normed = low(layer_norm(residual, norm_gain))
    gate_pair = low_back(matmul(normed, w_in.reshape(D, 2 * D))).reshape(row_count, 2, D)
    mixed_rows = glu_depth(gate_pair, kernel, row_count // LEN)
    mean_vec = lax.optimization_barrier(jnp.mean(mixed_rows, axis=0))
    centred = mixed_rows - mean_vec
    var_vec = lax.optimization_barrier(jnp.mean(centred * centred, axis=0))
    batch_out = centred * lax.rsqrt(var_vec + EPS) * scale_vec + shift_vec
    activated = low(jax.nn.silu(batch_out))
    return residual + low_back(matmul(activated, w_out))

def forward(tokens, ff_in, ff_out, att_qkv, att_pos, att_bias, att_out, conv_in, conv_depth, conv_out, gains):
    residual = tokens
    for layer_index in range(LAYERS):
        gain_rows = gains[layer_index]
        residual = feed_forward(residual, ff_in[layer_index, 0], ff_out[layer_index, 0], gain_rows[0])
        residual = attention(residual, att_qkv[layer_index], att_pos[layer_index], att_bias[layer_index], att_out[layer_index], gain_rows[1])
        residual = convolution(residual, conv_in[layer_index], conv_depth[layer_index], conv_out[layer_index], gain_rows[2], gain_rows[5], gain_rows[6])
        residual = feed_forward(residual, ff_in[layer_index, 1], ff_out[layer_index, 1], gain_rows[3])
        residual = layer_norm(residual, gain_rows[4])
    return residual

def reference(tokens, ff_in, ff_out, att_qkv, att_pos, att_bias, att_out, conv_in, conv_depth, conv_out, gains, out_grad):
    block_out, pullback = jax.vjp(forward, tokens.astype(jnp.float32), ff_in.astype(jnp.float32), ff_out.astype(jnp.float32), att_qkv.astype(jnp.float32), att_pos.astype(jnp.float32), att_bias.astype(jnp.float32), att_out.astype(jnp.float32), conv_in.astype(jnp.float32), conv_depth.astype(jnp.float32), conv_out.astype(jnp.float32), gains.astype(jnp.float32))
    grads = pullback(out_grad.astype(jnp.float32))
    return (block_out, grads[0], grads[1], grads[2], grads[3], grads[4], grads[5], grads[6], grads[7], grads[8], grads[9], grads[10])
```

```python
import math

import jax
import jax.numpy as jnp
from jax import lax
from jax.experimental import pallas as pl
from jax.experimental.pallas import tpu as pltpu
from jax.sharding import PartitionSpec as P

DH = 64
EPS = 1e-05
AXES = ("dp", "tensor")
BLOCK = 128
PAIR = 128
F32 = jnp.float32
BF16 = jnp.bfloat16


def matmul(left, right):
    return jnp.dot(left, right, preferred_element_type=F32)


def inner_rows(left, right):
    return lax.dot_general(left, right, (((0,), (0,)), ((), ())), preferred_element_type=F32)


def outer_cols(left, right):
    return lax.dot_general(left, right, (((1,), (1,)), ((), ())), preferred_element_type=F32)


def norm_parts(inputs):
    centre = inputs - jnp.mean(inputs, axis=-1, keepdims=True)
    inverse = lax.rsqrt(jnp.mean(centre * centre, axis=-1, keepdims=True) + EPS)
    return centre * inverse, inverse


def layer_norm(inputs, gain):
    return norm_parts(inputs)[0] * gain


def norm_back(inputs, gain, upstream):
    unit, inverse = norm_parts(inputs)
    scaled = upstream * gain
    mean_scaled = jnp.mean(scaled, axis=-1, keepdims=True)
    mean_product = jnp.mean(scaled * unit, axis=-1, keepdims=True)
    grad = inverse * (scaled - mean_scaled - unit * mean_product)
    return grad, jnp.sum(upstream * unit, axis=0)


def silu_slope(values):
    gate = jax.nn.sigmoid(values)
    return gate * (1.0 + values * (1.0 - gate))


def head_mask(head, scale):
    lanes = lax.broadcasted_iota(jnp.int32, (1, PAIR), 1)
    return jnp.where(lanes // DH == head, scale, 0.0).astype(BF16)


def padded_table(padded, model_width):
    distance = (padded - 1 - lax.broadcasted_iota(jnp.int32, (2 * padded, 1), 0)).astype(F32)
    columns = lax.broadcasted_iota(jnp.int32, (1, model_width), 1)
    frequency = jnp.exp((columns // 2).astype(F32) * (-2.0 * math.log(10000.0) / model_width))
    angles = distance * frequency
    return jnp.where(columns % 2 == 0, jnp.sin(angles), jnp.cos(angles)).astype(BF16)


def attend_forward(query_a, query_b, key_rows, value_rows, pos_keys, length):
    padded, width = key_rows.shape
    span = padded + BLOCK

    def kernel(qa_ref, qb_ref, k_ref, v_ref, pk_ref, out_ref, probs_ref):
        columns = lax.broadcasted_iota(jnp.int32, (BLOCK, padded), 1)

        def one_block(block, carry):
            rows = pl.ds(pl.multiple_of(block * BLOCK, BLOCK), BLOCK)
            near = pl.ds(pl.multiple_of(padded - BLOCK - block * BLOCK, BLOCK), span)
            total = jnp.zeros((BLOCK, PAIR), F32)
            for head in range(2):
                scale = head_mask(head, DH ** (-0.5))
                content = outer_cols(qa_ref[rows, :] * scale, k_ref[...])
                position = outer_cols(qb_ref[rows, :] * scale, pk_ref[near, :])
                position = pltpu.roll(
                    position, span - BLOCK + 1, 1, stride=1, stride_axis=0
                )[:, :padded]
                scores = jnp.where(columns < length, content + position, -1e30)
                weights = jnp.exp(scores - jnp.max(scores, axis=-1, keepdims=True))
                inverse = 1.0 / jnp.sum(weights, axis=-1, keepdims=True)
                probs = (weights * inverse).astype(BF16)
                probs_ref[head, rows, :] = probs
                total += matmul(probs, v_ref[...] * head_mask(head, 1.0))
            out_ref[rows, :] = total.astype(BF16)
            return carry

        lax.fori_loop(0, padded // BLOCK, one_block, 0)

    rows_spec = pl.BlockSpec((padded, PAIR), lambda pair: (0, pair))
    return pl.pallas_call(
        kernel,
        grid=(width // PAIR,),
        in_specs=[rows_spec] * 4 + [pl.BlockSpec((2 * padded, PAIR), lambda pair: (0, pair))],
        out_specs=[rows_spec, pl.BlockSpec((2, padded, padded), lambda pair: (pair, 0, 0))],
        out_shape=[
            jax.ShapeDtypeStruct((padded, width), BF16),
            jax.ShapeDtypeStruct((width // DH, padded, padded), BF16),
        ],
        compiler_params=pltpu.CompilerParams(vmem_limit_bytes=40 * 2**20),
        name="attend_forward",
    )(query_a, query_b, key_rows, value_rows, pos_keys)


def attend_backward(query_a, query_b, key_rows, value_rows, pos_keys, probs, attn_grad):
    padded, width = key_rows.shape
    span = padded + BLOCK

    def kernel(
        qa_ref, qb_ref, k_ref, v_ref, pk_ref, probs_ref, grad_ref,
        dq_ref, dk_ref, dv_ref, dpk_ref, bias_ref,
        dk_acc, dv_acc, dpk_acc,
    ):
        dk_acc[...] = jnp.zeros_like(dk_acc)
        dv_acc[...] = jnp.zeros_like(dv_acc)
        dpk_acc[...] = jnp.zeros_like(dpk_acc)
        row_ids = lax.broadcasted_iota(jnp.int32, (BLOCK, BLOCK), 0)
        col_ids = lax.broadcasted_iota(jnp.int32, (BLOCK, BLOCK), 1)
        flip_f = jnp.where(row_ids + col_ids == BLOCK - 1, 1.0, 0.0)
        flip = flip_f.astype(BF16)

        def one_block(block, sums):
            sum_a, sum_b = sums
            rows = pl.ds(pl.multiple_of(block * BLOCK, BLOCK), BLOCK)
            near = pl.ds(pl.multiple_of(padded - BLOCK - block * BLOCK, BLOCK), span)
            qa, qb, grad = qa_ref[rows, :], qb_ref[rows, :], grad_ref[rows, :]
            qb_flip = matmul(flip, qb).astype(BF16)
            dqa = jnp.zeros((BLOCK, PAIR), F32)
            dqb_flip = jnp.zeros((BLOCK, PAIR), F32)
            for head in range(2):
                mask = head_mask(head, 1.0)
                probs_low = probs_ref[head, rows, :]
                probs_f = probs_low.astype(F32)
                prob_grad = outer_cols(grad * head_mask(head, DH ** (-0.5)), v_ref[...])
                product = probs_f * prob_grad
                centre = jnp.sum(product, axis=-1, keepdims=True)
                score_grad = (product - probs_f * centre).astype(BF16)
                dqa += matmul(score_grad, k_ref[...] * mask)
                dk_acc[...] += inner_rows(qa * mask, score_grad)
                dv_acc[...] += inner_rows(grad * mask, probs_low)
                flipped = matmul(flip, score_grad)
                wide = jnp.concatenate([flipped, jnp.zeros((BLOCK, BLOCK), F32)], axis=1)
                position_grad = pltpu.roll(wide, 0, 1, stride=1, stride_axis=0).astype(BF16)
                dqb_flip += matmul(position_grad, pk_ref[near, :] * mask)
                dpk_acc[:, near] += inner_rows(qb_flip * mask, position_grad)
            dqb = lax.dot_general(
                flip_f, dqb_flip, (((1,), (0,)), ((), ())),
                precision=lax.Precision.HIGHEST, preferred_element_type=F32,
            )
            dq_ref[rows, :] = (dqa + dqb).astype(BF16)
            return (
                sum_a + jnp.sum(dqa, axis=0, keepdims=True),
                sum_b + jnp.sum(dqb_flip, axis=0, keepdims=True),
            )

        start = jnp.zeros((1, PAIR), F32)
        sum_a, sum_b = lax.fori_loop(0, padded // BLOCK, one_block, (start, start))
        bias_ref[...] = jnp.concatenate([sum_a, sum_b, jnp.zeros((6, PAIR), F32)], axis=0)
        dk_ref[...] = dk_acc[...].T.astype(BF16)
        dv_ref[...] = dv_acc[...].T.astype(BF16)
        dpk_ref[...] = dpk_acc[...].T.astype(BF16)

    rows_spec = pl.BlockSpec((padded, PAIR), lambda pair: (0, pair))
    wide_spec = pl.BlockSpec((2 * padded, PAIR), lambda pair: (0, pair))
    return pl.pallas_call(
        kernel,
        grid=(width // PAIR,),
        in_specs=[rows_spec] * 4
        + [wide_spec, pl.BlockSpec((2, padded, padded), lambda pair: (pair, 0, 0)), rows_spec],
        out_specs=[rows_spec] * 3 + [wide_spec, pl.BlockSpec((8, PAIR), lambda pair: (0, pair))],
        out_shape=[jax.ShapeDtypeStruct((padded, width), BF16)] * 3
        + [
            jax.ShapeDtypeStruct((2 * padded, width), BF16),
            jax.ShapeDtypeStruct((8, width), F32),
        ],
        scratch_shapes=[
            pltpu.VMEM((PAIR, padded), F32),
            pltpu.VMEM((PAIR, padded), F32),
            pltpu.VMEM((PAIR, 2 * padded), F32),
        ],
        compiler_params=pltpu.CompilerParams(vmem_limit_bytes=40 * 2**20),
        name="attend_backward",
    )(query_a, query_b, key_rows, value_rows, pos_keys, probs, attn_grad)


ROWS = 64


def depthwise(signal, taps):
    out_rows, width = signal.shape[0] - 32, signal.shape[1]

    def kernel(signal_ref, taps_ref, out_ref):
        def one_chunk(chunk, carry):
            base = pl.multiple_of(chunk * ROWS, ROWS)
            total = jnp.zeros((ROWS, 128), F32)
            for tap in range(31):
                total += signal_ref[pl.ds(base + tap, ROWS), :] * taps_ref[tap : tap + 1, :]
            out_ref[pl.ds(base, ROWS), :] = total
            return carry

        lax.fori_loop(0, out_rows // ROWS, one_chunk, 0)

    return pl.pallas_call(
        kernel,
        grid=(width // 128,),
        in_specs=[
            pl.BlockSpec((out_rows + 32, 128), lambda part: (0, part)),
            pl.BlockSpec((32, 128), lambda part: (0, part)),
        ],
        out_specs=pl.BlockSpec((out_rows, 128), lambda part: (0, part)),
        out_shape=jax.ShapeDtypeStruct((out_rows, width), F32),
        name="depthwise",
    )(signal, taps)


def depthwise_taps(signal, upstream):
    out_rows, width = upstream.shape

    def kernel(signal_ref, up_ref, out_ref):
        def one_chunk(chunk, totals):
            base = pl.multiple_of(chunk * ROWS, ROWS)
            grad = up_ref[pl.ds(base, ROWS), :]
            result = []
            for tap in range(31):
                product = signal_ref[pl.ds(base + tap, ROWS), :] * grad
                result.append(
                    totals[tap] + jnp.sum(product.reshape(ROWS // 8, 8, 128), axis=0)
                )
            return tuple(result)

        start = tuple(jnp.zeros((8, 128), F32) for _ in range(31))
        totals = lax.fori_loop(0, out_rows // ROWS, one_chunk, start)
        for tap in range(31):
            out_ref[tap : tap + 1, :] = jnp.sum(totals[tap], axis=0, keepdims=True)
        out_ref[31:32, :] = jnp.zeros((1, 128), F32)

    return pl.pallas_call(
        kernel,
        grid=(width // 128,),
        in_specs=[
            pl.BlockSpec((out_rows + 32, 128), lambda part: (0, part)),
            pl.BlockSpec((out_rows, 128), lambda part: (0, part)),
        ],
        out_specs=pl.BlockSpec((32, 128), lambda part: (0, part)),
        out_shape=jax.ShapeDtypeStruct((32, width), F32),
        name="depthwise_taps",
    )(signal, upstream)


def local(
    tokens, ff_in, ff_out, att_qkv, att_pos, att_bias, att_out,
    conv_in, conv_depth, conv_out, gains, out_grad,
):
    length, width = tokens.shape
    dp, tp = lax.axis_size("dp"), lax.axis_size("tensor")
    count = dp * tp
    total_rows = length * count
    padded = -(-length // BLOCK) * BLOCK
    piece = width // count
    units = ff_in.shape[3]
    in_rows, half = att_pos.shape[1], att_pos.shape[2]
    bias_heads, bias_width = att_bias.shape[1], att_bias.shape[2]
    heads = bias_heads * tp
    tap_count = conv_depth.shape[1]
    margin = (tap_count - 1) // 2

    def gather(array):
        return lax.all_gather(array, AXES, axis=0)

    def scatter(array):
        return lax.psum_scatter(array, AXES, scatter_dimension=0, tiled=False)

    small = jnp.concatenate(
        [
            gains[0].reshape(-1),
            conv_depth[0].astype(F32).reshape(-1),
            att_bias[0].astype(F32).reshape(-1),
        ]
    )
    ff_first = gather(jnp.concatenate([ff_in[0, 0].T, ff_out[0, 0]], axis=0))
    small = gather(small)
    att_all = gather(
        jnp.concatenate([att_qkv[0].reshape(-1, half), att_pos[0], att_out[0].T], axis=0)
    )
    rest_all = gather(
        jnp.concatenate(
            [
                conv_in[0].transpose(1, 2, 0).reshape(2 * piece, width),
                conv_out[0],
                ff_in[0, 1].T,
                ff_out[0, 1],
            ],
            axis=0,
        )
    )
    gain_end, depth_end = 7 * piece, (7 + tap_count) * piece
    gain_rows = small[:, :gain_end].reshape(count, 7, piece).transpose(1, 0, 2).reshape(7, width)
    taps = (
        small[:, gain_end:depth_end]
        .reshape(count, tap_count, piece)
        .transpose(1, 0, 2)
        .reshape(tap_count, width)
    )
    bias = (
        small[:, depth_end:]
        .reshape(dp, tp, bias_heads, bias_width)
        .transpose(1, 2, 0, 3)
        .reshape(heads, 2 * DH)
    )
    w_in_t = [ff_first[:, :units].reshape(-1, width)]
    w_out = [ff_first[:, units:].reshape(-1, width)]
    att_all = att_all.reshape(dp, tp, 5 * in_rows, half)
    w_qkv = (
        att_all[:, :, : 3 * in_rows]
        .reshape(dp, tp, in_rows, 3, half)
        .transpose(0, 2, 3, 1, 4)
        .reshape(width, 3 * width)
    )
    w_pos = att_all[:, :, 3 * in_rows : 4 * in_rows].transpose(0, 2, 1, 3).reshape(width, width)
    w_aout_t = att_all[:, :, 4 * in_rows :].transpose(0, 2, 1, 3).reshape(width, width)
    w_cin_t = (
        rest_all[:, : 2 * piece]
        .reshape(count, 2, piece, width)
        .transpose(1, 0, 2, 3)
        .reshape(2 * width, width)
    )
    w_cout = rest_all[:, 2 * piece : 3 * piece].reshape(width, width)
    w_in_t.append(rest_all[:, 3 * piece : 3 * piece + units].reshape(-1, width))
    w_out.append(rest_all[:, 3 * piece + units :].reshape(-1, width))

    def mlp_forward(residual, module, gain):
        normed = layer_norm(residual, gain).astype(BF16)
        hidden_pre = outer_cols(normed, w_in_t[module])
        hidden = jax.nn.silu(hidden_pre).astype(BF16)
        return residual + 0.5 * matmul(hidden, w_out[module]), (normed, hidden_pre, hidden)

    def mlp_backward(residual, upstream, stored, module, gain):
        normed, hidden_pre, hidden = stored
        branch_grad = (0.5 * upstream).astype(BF16)
        hidden_grad = outer_cols(branch_grad, w_out[module])
        pre_grad = (hidden_grad * silu_slope(hidden_pre)).astype(BF16)
        out_grad_rows = inner_rows(hidden, branch_grad).astype(BF16)
        in_grad_rows = inner_rows(pre_grad, normed).astype(BF16)
        normed_grad = matmul(pre_grad, w_in_t[module])
        residual_grad, gain_grad = norm_back(residual, gain, normed_grad)
        terms = [
            in_grad_rows.reshape(count, units, width),
            out_grad_rows.reshape(count, units, width),
        ]
        return upstream + residual_grad, terms, gain_grad

    def pad_rows(array):
        return jnp.pad(array, ((0, padded - length), (0, 0)))

    residual_0 = tokens.astype(F32)
    residual_1, first_ff = mlp_forward(residual_0, 0, gain_rows[0])

    att_normed = layer_norm(residual_1, gain_rows[1]).astype(BF16)
    packed = matmul(att_normed, w_qkv)
    query = packed[:, :width]
    query_a = pad_rows((query + bias[:, :DH].reshape(-1)).astype(BF16))
    query_b = pad_rows((query + bias[:, DH:].reshape(-1)).astype(BF16))
    key_rows = pad_rows(packed[:, width : 2 * width].astype(BF16))
    value_rows = pad_rows(packed[:, 2 * width :].astype(BF16))
    pos_table = padded_table(padded, width)
    pos_keys = matmul(pos_table, w_pos).astype(BF16)
    attended, probs = attend_forward(query_a, query_b, key_rows, value_rows, pos_keys, length)
    attended = attended[:length]
    residual_2 = residual_1 + outer_cols(attended, w_aout_t)

    conv_normed = layer_norm(residual_2, gain_rows[2]).astype(BF16)
    gate_pair = outer_cols(conv_normed, w_cin_t)
    value_part, gate = gate_pair[:, :width], jax.nn.sigmoid(gate_pair[:, width:])
    conv_pad = ((margin, padded + 32 - margin - length), (0, 0))
    glu = jnp.pad(value_part * gate, conv_pad)
    taps_pad = jnp.pad(taps, ((0, 32 - tap_count), (0, 0)))
    taps_back = jnp.pad(taps[::-1], ((0, 32 - tap_count), (0, 0)))
    mixed_rows = depthwise(glu, taps_pad)[:length]
    own_mean = jnp.mean(mixed_rows, axis=0)
    own_square = jnp.sum((mixed_rows - own_mean) ** 2, axis=0)
    moments = gather(jnp.stack([own_mean, own_square]))
    mean_vec = jnp.mean(moments[:, 0], axis=0)
    var_vec = (
        jnp.sum(moments[:, 1], axis=0) + length * jnp.sum((moments[:, 0] - mean_vec) ** 2, axis=0)
    ) / total_rows
    inv_std = lax.rsqrt(var_vec + EPS)
    normal_rows = (mixed_rows - mean_vec) * inv_std
    batch_out = normal_rows * gain_rows[5] + gain_rows[6]
    activated = jax.nn.silu(batch_out).astype(BF16)
    residual_3 = residual_2 + matmul(activated, w_cout)

    residual_4, second_ff = mlp_forward(residual_3, 1, gain_rows[3])
    block_out = layer_norm(residual_4, gain_rows[4])

    upstream, final_gain = norm_back(residual_4, gain_rows[4], out_grad)
    upstream, second_terms, second_gain = mlp_backward(
        residual_3, upstream, second_ff, 1, gain_rows[3]
    )
    second_sum = scatter(jnp.concatenate(second_terms, axis=1))

    branch_grad = upstream.astype(BF16)
    act_grad = outer_cols(branch_grad, w_cout)
    cout_terms = inner_rows(activated, branch_grad).astype(BF16).reshape(count, piece, width)
    batch_grad = act_grad * silu_slope(batch_out)
    shift_part = jnp.sum(batch_grad, axis=0)
    scale_part = jnp.sum(batch_grad * normal_rows, axis=0)
    totals = jnp.sum(gather(jnp.stack([scale_part, shift_part])), axis=0)
    mixed_grad = (
        gain_rows[5]
        * inv_std
        * (batch_grad - totals[1] / total_rows - normal_rows * (totals[0] / total_rows))
    )
    mixed_pad = jnp.pad(mixed_grad, conv_pad)
    glu_grad = depthwise(mixed_pad, taps_back)[:length]
    depth_grad = depthwise_taps(glu, pad_rows(mixed_grad))[:tap_count]
    pair_grad = jnp.concatenate(
        [glu_grad * gate, glu_grad * value_part * gate * (1.0 - gate)], axis=1
    ).astype(BF16)
    cin_terms = (
        inner_rows(pair_grad, conv_normed)
        .astype(BF16)
        .reshape(2, count, piece, width)
        .transpose(1, 0, 2, 3)
        .reshape(count, 2 * piece, width)
    )
    conv_sum = scatter(jnp.concatenate([cin_terms, cout_terms], axis=1))
    residual_grad, conv_gain = norm_back(residual_2, gain_rows[2], matmul(pair_grad, w_cin_t))
    upstream = upstream + residual_grad

    branch_grad = upstream.astype(BF16)
    attn_grad = pad_rows(matmul(branch_grad, w_aout_t).astype(BF16))
    aout_terms = inner_rows(branch_grad, attended)
    query_grad, key_grad, value_grad, pos_grad, bias_sums = attend_backward(
        query_a, query_b, key_rows, value_rows, pos_keys, probs, attn_grad
    )
    pack_grad = jnp.concatenate([query_grad, key_grad, value_grad], axis=1)[:length]
    qkv_terms = inner_rows(att_normed, pack_grad)
    pos_terms = inner_rows(pos_table, pos_grad)

    def square_terms(array):
        shaped = array.astype(BF16).reshape(dp, in_rows, tp, half).transpose(0, 2, 1, 3)
        return shaped.reshape(count, in_rows, half)

    qkv_terms = (
        qkv_terms.astype(BF16)
        .reshape(dp, in_rows, 3, tp, half)
        .transpose(0, 3, 1, 2, 4)
        .reshape(count, 3 * in_rows, half)
    )
    att_sum = scatter(
        jnp.concatenate([qkv_terms, square_terms(pos_terms), square_terms(aout_terms)], axis=1)
    )
    residual_grad, attend_gain = norm_back(
        residual_1, gain_rows[1], outer_cols(pack_grad, w_qkv)
    )
    upstream = upstream + residual_grad

    tokens_grad, first_terms, first_gain = mlp_backward(
        residual_0, upstream, first_ff, 0, gain_rows[0]
    )
    first_sum = scatter(jnp.concatenate(first_terms, axis=1))

    gain_terms = jnp.stack(
        [first_gain, attend_gain, conv_gain, second_gain, final_gain, scale_part, shift_part]
    )
    bias_terms = jnp.concatenate(
        [bias_sums[0].reshape(heads, DH), bias_sums[1].reshape(heads, DH)], axis=1
    )
    small_terms = jnp.concatenate(
        [
            gain_terms.reshape(7, count, piece).transpose(1, 0, 2).reshape(count, -1),
            depth_grad.reshape(tap_count, count, piece).transpose(1, 0, 2).reshape(count, -1),
            bias_terms.reshape(tp, bias_heads, dp, bias_width)
            .transpose(2, 0, 1, 3)
            .reshape(count, -1),
        ],
        axis=1,
    )
    small_sum = scatter(small_terms)

    first_sum, second_sum = first_sum.astype(F32), second_sum.astype(F32)
    conv_sum, att_sum = conv_sum.astype(F32), att_sum.astype(F32)
    return (
        block_out,
        tokens_grad,
        jnp.stack([first_sum[:units].T, second_sum[:units].T])[None],
        jnp.stack([first_sum[units:], second_sum[units:]])[None],
        att_sum[: 3 * in_rows].reshape(1, in_rows, 3, half),
        att_sum[3 * in_rows : 4 * in_rows][None],
        small_sum[depth_end:].reshape(1, bias_heads, bias_width),
        att_sum[4 * in_rows :].T[None],
        conv_sum[: 2 * piece].reshape(2, piece, width).transpose(2, 0, 1)[None],
        small_sum[gain_end:depth_end].reshape(1, tap_count, piece),
        conv_sum[2 * piece :][None],
        small_sum[:gain_end].reshape(1, 7, piece),
    )


def solution(mesh):
    placed = (
        P(AXES, None),
        P(None, None, None, AXES),
        P(None, None, AXES, None),
        P(None, "dp", None, "tensor"),
        P(None, "dp", "tensor"),
        P(None, "tensor", "dp"),
        P(None, "tensor", "dp"),
        P(None, None, None, AXES),
        P(None, None, AXES),
        P(None, AXES, None),
        P(None, None, AXES),
        P(AXES, None),
    )
    return jax.shard_map(
        local,
        mesh=mesh,
        in_specs=placed,
        out_specs=(P(AXES, None),) + placed[:11],
        check_vma=False,
    )
```

```python
import math

import jax
import jax.numpy as jnp
from jax import lax
from jax.experimental import pallas as pl
from jax.experimental.pallas import tpu as pltpu
from jax.sharding import PartitionSpec as P

DH = 64
EPS = 1e-05
AXES = ("dp", "tensor")
BLOCK = 128
PAIR = 128
F32 = jnp.float32
BF16 = jnp.bfloat16


def matmul(left, right):
    return jnp.dot(left, right, preferred_element_type=F32)


def inner_rows(left, right):
    return lax.dot_general(left, right, (((0,), (0,)), ((), ())), preferred_element_type=F32)


def outer_cols(left, right):
    return lax.dot_general(left, right, (((1,), (1,)), ((), ())), preferred_element_type=F32)


def norm_parts(inputs):
    centre = inputs - jnp.mean(inputs, axis=-1, keepdims=True)
    inverse = lax.rsqrt(jnp.mean(centre * centre, axis=-1, keepdims=True) + EPS)
    return centre * inverse, inverse


def layer_norm(inputs, gain):
    return norm_parts(inputs)[0] * gain


def norm_back(inputs, gain, upstream):
    unit, inverse = norm_parts(inputs)
    scaled = upstream * gain
    mean_scaled = jnp.mean(scaled, axis=-1, keepdims=True)
    mean_product = jnp.mean(scaled * unit, axis=-1, keepdims=True)
    grad = inverse * (scaled - mean_scaled - unit * mean_product)
    return grad, jnp.sum(upstream * unit, axis=0)


def silu_slope(values):
    gate = jax.nn.sigmoid(values)
    return gate * (1.0 + values * (1.0 - gate))


def head_mask(head, scale):
    lanes = lax.broadcasted_iota(jnp.int32, (1, PAIR), 1)
    return jnp.where(lanes // DH == head, scale, 0.0).astype(BF16)


def padded_table(padded, model_width):
    distance = (padded - 1 - lax.broadcasted_iota(jnp.int32, (2 * padded, 1), 0)).astype(F32)
    columns = lax.broadcasted_iota(jnp.int32, (1, model_width), 1)
    frequency = jnp.exp((columns // 2).astype(F32) * (-2.0 * math.log(10000.0) / model_width))
    angles = distance * frequency
    return jnp.where(columns % 2 == 0, jnp.sin(angles), jnp.cos(angles)).astype(BF16)


def attend_forward(query_a, query_b, key_rows, value_rows, pos_keys, length):
    padded, width = key_rows.shape
    span = padded + BLOCK

    def kernel(qa_ref, qb_ref, k_ref, v_ref, pk_ref, out_ref, probs_ref):
        columns = lax.broadcasted_iota(jnp.int32, (BLOCK, padded), 1)

        def one_block(block, carry):
            rows = pl.ds(pl.multiple_of(block * BLOCK, BLOCK), BLOCK)
            near = pl.ds(pl.multiple_of(padded - BLOCK - block * BLOCK, BLOCK), span)
            total = jnp.zeros((BLOCK, PAIR), F32)
            for head in range(2):
                scale = head_mask(head, DH ** (-0.5))
                content = outer_cols(qa_ref[rows, :] * scale, k_ref[...])
                position = outer_cols(qb_ref[rows, :] * scale, pk_ref[near, :])
                position = pltpu.roll(
                    position, span - BLOCK + 1, 1, stride=1, stride_axis=0
                )[:, :padded]
                scores = jnp.where(columns < length, content + position, -1e30)
                weights = jnp.exp(scores - jnp.max(scores, axis=-1, keepdims=True))
                inverse = 1.0 / jnp.sum(weights, axis=-1, keepdims=True)
                probs = (weights * inverse).astype(BF16)
                probs_ref[head, rows, :] = probs
                total += matmul(probs, v_ref[...] * head_mask(head, 1.0))
            out_ref[rows, :] = total.astype(BF16)
            return carry

        lax.fori_loop(0, padded // BLOCK, one_block, 0)

    rows_spec = pl.BlockSpec((padded, PAIR), lambda pair: (0, pair))
    return pl.pallas_call(
        kernel,
        grid=(width // PAIR,),
        in_specs=[rows_spec] * 4 + [pl.BlockSpec((2 * padded, PAIR), lambda pair: (0, pair))],
        out_specs=[rows_spec, pl.BlockSpec((2, padded, padded), lambda pair: (pair, 0, 0))],
        out_shape=[
            jax.ShapeDtypeStruct((padded, width), BF16),
            jax.ShapeDtypeStruct((width // DH, padded, padded), BF16),
        ],
        compiler_params=pltpu.CompilerParams(vmem_limit_bytes=40 * 2**20),
        name="attend_forward",
    )(query_a, query_b, key_rows, value_rows, pos_keys)


def attend_backward(query_a, query_b, key_rows, value_rows, pos_keys, probs, attn_grad):
    padded, width = key_rows.shape
    span = padded + BLOCK

    def kernel(
        qa_ref, qb_ref, k_ref, v_ref, pk_ref, probs_ref, grad_ref,
        dq_ref, dk_ref, dv_ref, dpk_ref, bias_ref,
        dk_acc, dv_acc, dpk_acc,
    ):
        dk_acc[...] = jnp.zeros_like(dk_acc)
        dv_acc[...] = jnp.zeros_like(dv_acc)
        dpk_acc[...] = jnp.zeros_like(dpk_acc)
        row_ids = lax.broadcasted_iota(jnp.int32, (BLOCK, BLOCK), 0)
        col_ids = lax.broadcasted_iota(jnp.int32, (BLOCK, BLOCK), 1)
        flip_f = jnp.where(row_ids + col_ids == BLOCK - 1, 1.0, 0.0)
        flip = flip_f.astype(BF16)

        def one_block(block, sums):
            sum_a, sum_b = sums
            rows = pl.ds(pl.multiple_of(block * BLOCK, BLOCK), BLOCK)
            near = pl.ds(pl.multiple_of(padded - BLOCK - block * BLOCK, BLOCK), span)
            qa, qb, grad = qa_ref[rows, :], qb_ref[rows, :], grad_ref[rows, :]
            qb_flip = matmul(flip, qb).astype(BF16)
            dqa = jnp.zeros((BLOCK, PAIR), F32)
            dqb_flip = jnp.zeros((BLOCK, PAIR), F32)
            for head in range(2):
                mask = head_mask(head, 1.0)
                probs_low = probs_ref[head, rows, :]
                probs_f = probs_low.astype(F32)
                prob_grad = outer_cols(grad * head_mask(head, DH ** (-0.5)), v_ref[...])
                product = probs_f * prob_grad
                centre = jnp.sum(product, axis=-1, keepdims=True)
                score_grad = (product - probs_f * centre).astype(BF16)
                dqa += matmul(score_grad, k_ref[...] * mask)
                dk_acc[...] += inner_rows(qa * mask, score_grad)
                dv_acc[...] += inner_rows(grad * mask, probs_low)
                flipped = matmul(flip, score_grad)
                wide = jnp.concatenate([flipped, jnp.zeros((BLOCK, BLOCK), F32)], axis=1)
                position_grad = pltpu.roll(wide, 0, 1, stride=1, stride_axis=0).astype(BF16)
                dqb_flip += matmul(position_grad, pk_ref[near, :] * mask)
                dpk_acc[:, near] += inner_rows(qb_flip * mask, position_grad)
            dqb = lax.dot_general(
                flip_f, dqb_flip, (((1,), (0,)), ((), ())),
                precision=lax.Precision.HIGHEST, preferred_element_type=F32,
            )
            dq_ref[rows, :] = (dqa + dqb).astype(BF16)
            return (
                sum_a + jnp.sum(dqa, axis=0, keepdims=True),
                sum_b + jnp.sum(dqb_flip, axis=0, keepdims=True),
            )

        start = jnp.zeros((1, PAIR), F32)
        sum_a, sum_b = lax.fori_loop(0, padded // BLOCK, one_block, (start, start))
        bias_ref[...] = jnp.concatenate([sum_a, sum_b, jnp.zeros((6, PAIR), F32)], axis=0)
        dk_ref[...] = dk_acc[...].T.astype(BF16)
        dv_ref[...] = dv_acc[...].T.astype(BF16)
        dpk_ref[...] = dpk_acc[...].T.astype(BF16)

    rows_spec = pl.BlockSpec((padded, PAIR), lambda pair: (0, pair))
    wide_spec = pl.BlockSpec((2 * padded, PAIR), lambda pair: (0, pair))
    return pl.pallas_call(
        kernel,
        grid=(width // PAIR,),
        in_specs=[rows_spec] * 4
        + [wide_spec, pl.BlockSpec((2, padded, padded), lambda pair: (pair, 0, 0)), rows_spec],
        out_specs=[rows_spec] * 3 + [wide_spec, pl.BlockSpec((8, PAIR), lambda pair: (0, pair))],
        out_shape=[jax.ShapeDtypeStruct((padded, width), BF16)] * 3
        + [
            jax.ShapeDtypeStruct((2 * padded, width), BF16),
            jax.ShapeDtypeStruct((8, width), F32),
        ],
        scratch_shapes=[
            pltpu.VMEM((PAIR, padded), F32),
            pltpu.VMEM((PAIR, padded), F32),
            pltpu.VMEM((PAIR, 2 * padded), F32),
        ],
        compiler_params=pltpu.CompilerParams(vmem_limit_bytes=40 * 2**20),
        name="attend_backward",
    )(query_a, query_b, key_rows, value_rows, pos_keys, probs, attn_grad)


ROWS = 64


def depthwise(signal, taps):
    out_rows, width = signal.shape[0] - 32, signal.shape[1]

    def kernel(signal_ref, taps_ref, out_ref):
        def one_chunk(chunk, carry):
            base = pl.multiple_of(chunk * ROWS, ROWS)
            total = jnp.zeros((ROWS, 128), F32)
            for tap in range(31):
                total += signal_ref[pl.ds(base + tap, ROWS), :] * taps_ref[tap : tap + 1, :]
            out_ref[pl.ds(base, ROWS), :] = total
            return carry

        lax.fori_loop(0, out_rows // ROWS, one_chunk, 0)

    return pl.pallas_call(
        kernel,
        grid=(width // 128,),
        in_specs=[
            pl.BlockSpec((out_rows + 32, 128), lambda part: (0, part)),
            pl.BlockSpec((32, 128), lambda part: (0, part)),
        ],
        out_specs=pl.BlockSpec((out_rows, 128), lambda part: (0, part)),
        out_shape=jax.ShapeDtypeStruct((out_rows, width), F32),
        name="depthwise",
    )(signal, taps)


def depthwise_taps(signal, upstream):
    out_rows, width = upstream.shape

    def kernel(signal_ref, up_ref, out_ref):
        def one_chunk(chunk, totals):
            base = pl.multiple_of(chunk * ROWS, ROWS)
            grad = up_ref[pl.ds(base, ROWS), :]
            result = []
            for tap in range(31):
                product = signal_ref[pl.ds(base + tap, ROWS), :] * grad
                result.append(
                    totals[tap] + jnp.sum(product.reshape(ROWS // 8, 8, 128), axis=0)
                )
            return tuple(result)

        start = tuple(jnp.zeros((8, 128), F32) for _ in range(31))
        totals = lax.fori_loop(0, out_rows // ROWS, one_chunk, start)
        for tap in range(31):
            out_ref[tap : tap + 1, :] = jnp.sum(totals[tap], axis=0, keepdims=True)
        out_ref[31:32, :] = jnp.zeros((1, 128), F32)

    return pl.pallas_call(
        kernel,
        grid=(width // 128,),
        in_specs=[
            pl.BlockSpec((out_rows + 32, 128), lambda part: (0, part)),
            pl.BlockSpec((out_rows, 128), lambda part: (0, part)),
        ],
        out_specs=pl.BlockSpec((32, 128), lambda part: (0, part)),
        out_shape=jax.ShapeDtypeStruct((32, width), F32),
        name="depthwise_taps",
    )(signal, upstream)


def local(
    tokens, ff_in, ff_out, att_qkv, att_pos, att_bias, att_out,
    conv_in, conv_depth, conv_out, gains, out_grad,
):
    length, width = tokens.shape
    dp, tp = lax.axis_size("dp"), lax.axis_size("tensor")
    count = dp * tp
    total_rows = length * count
    padded = -(-length // BLOCK) * BLOCK
    piece = width // count
    units = ff_in.shape[3]
    in_rows, half = att_pos.shape[1], att_pos.shape[2]
    bias_heads, bias_width = att_bias.shape[1], att_bias.shape[2]
    heads = bias_heads * tp
    tap_count = conv_depth.shape[1]
    margin = (tap_count - 1) // 2

    def gather(array):
        return lax.all_gather(array, AXES, axis=0)

    def scatter(array):
        return lax.psum_scatter(array, AXES, scatter_dimension=0, tiled=False)

    small = jnp.concatenate(
        [
            gains[0].reshape(-1),
            conv_depth[0].astype(F32).reshape(-1),
            att_bias[0].astype(F32).reshape(-1),
        ]
    )
    ff_first = gather(jnp.concatenate([ff_in[0, 0].T, ff_out[0, 0]], axis=0))
    small = gather(small)
    att_all = gather(
        jnp.concatenate([att_qkv[0].reshape(-1, half), att_pos[0], att_out[0].T], axis=0)
    )
    rest_all = gather(
        jnp.concatenate(
            [
                conv_in[0].transpose(1, 2, 0).reshape(2 * piece, width),
                conv_out[0],
                ff_in[0, 1].T,
                ff_out[0, 1],
            ],
            axis=0,
        )
    )
    gain_end, depth_end = 7 * piece, (7 + tap_count) * piece
    gain_rows = small[:, :gain_end].reshape(count, 7, piece).transpose(1, 0, 2).reshape(7, width)
    taps = (
        small[:, gain_end:depth_end]
        .reshape(count, tap_count, piece)
        .transpose(1, 0, 2)
        .reshape(tap_count, width)
    )
    bias = (
        small[:, depth_end:]
        .reshape(dp, tp, bias_heads, bias_width)
        .transpose(1, 2, 0, 3)
        .reshape(heads, 2 * DH)
    )
    w_in_t = [ff_first[:, :units].reshape(-1, width)]
    w_out = [ff_first[:, units:].reshape(-1, width)]
    att_all = att_all.reshape(dp, tp, 5 * in_rows, half)
    w_qkv = (
        att_all[:, :, : 3 * in_rows]
        .reshape(dp, tp, in_rows, 3, half)
        .transpose(0, 2, 3, 1, 4)
        .reshape(width, 3 * width)
    )
    w_pos = att_all[:, :, 3 * in_rows : 4 * in_rows].transpose(0, 2, 1, 3).reshape(width, width)
    w_aout_t = att_all[:, :, 4 * in_rows :].transpose(0, 2, 1, 3).reshape(width, width)
    w_cin_t = (
        rest_all[:, : 2 * piece]
        .reshape(count, 2, piece, width)
        .transpose(1, 0, 2, 3)
        .reshape(2 * width, width)
    )
    w_cout = rest_all[:, 2 * piece : 3 * piece].reshape(width, width)
    w_in_t.append(rest_all[:, 3 * piece : 3 * piece + units].reshape(-1, width))
    w_out.append(rest_all[:, 3 * piece + units :].reshape(-1, width))

    def mlp_forward(residual, module, gain):
        normed = layer_norm(residual, gain).astype(BF16)
        hidden_pre = outer_cols(normed, w_in_t[module])
        hidden = jax.nn.silu(hidden_pre).astype(BF16)
        return residual + 0.5 * matmul(hidden, w_out[module]), (normed, hidden_pre, hidden)

    def mlp_backward(residual, upstream, stored, module, gain):
        normed, hidden_pre, hidden = stored
        branch_grad = (0.5 * upstream).astype(BF16)
        hidden_grad = outer_cols(branch_grad, w_out[module])
        pre_grad = (hidden_grad * silu_slope(hidden_pre)).astype(BF16)
        out_grad_rows = inner_rows(hidden, branch_grad).astype(BF16)
        in_grad_rows = inner_rows(pre_grad, normed).astype(BF16)
        normed_grad = matmul(pre_grad, w_in_t[module])
        residual_grad, gain_grad = norm_back(residual, gain, normed_grad)
        terms = [
            in_grad_rows.reshape(count, units, width),
            out_grad_rows.reshape(count, units, width),
        ]
        return upstream + residual_grad, terms, gain_grad

    def pad_rows(array):
        return jnp.pad(array, ((0, padded - length), (0, 0)))

    residual_0 = tokens.astype(F32)
    residual_1, first_ff = mlp_forward(residual_0, 0, gain_rows[0])

    att_normed = layer_norm(residual_1, gain_rows[1]).astype(BF16)
    packed = matmul(att_normed, w_qkv)
    query = packed[:, :width]
    query_a = pad_rows((query + bias[:, :DH].reshape(-1)).astype(BF16))
    query_b = pad_rows((query + bias[:, DH:].reshape(-1)).astype(BF16))
    key_rows = pad_rows(packed[:, width : 2 * width].astype(BF16))
    value_rows = pad_rows(packed[:, 2 * width :].astype(BF16))
    pos_table = padded_table(padded, width)
    pos_keys = matmul(pos_table, w_pos).astype(BF16)
    attended, probs = attend_forward(query_a, query_b, key_rows, value_rows, pos_keys, length)
    attended = attended[:length]
    residual_2 = residual_1 + outer_cols(attended, w_aout_t)

    conv_normed = layer_norm(residual_2, gain_rows[2]).astype(BF16)
    gate_pair = outer_cols(conv_normed, w_cin_t)
    value_part, gate = gate_pair[:, :width], jax.nn.sigmoid(gate_pair[:, width:])
    conv_pad = ((margin, padded + 32 - margin - length), (0, 0))
    glu = jnp.pad(value_part * gate, conv_pad)
    taps_pad = jnp.pad(taps, ((0, 32 - tap_count), (0, 0)))
    taps_back = jnp.pad(taps[::-1], ((0, 32 - tap_count), (0, 0)))
    mixed_rows = depthwise(glu, taps_pad)[:length]
    own_mean = jnp.mean(mixed_rows, axis=0)
    own_square = jnp.sum((mixed_rows - own_mean) ** 2, axis=0)
    moments = gather(jnp.stack([own_mean, own_square]))
    mean_vec = jnp.mean(moments[:, 0], axis=0)
    var_vec = (
        jnp.sum(moments[:, 1], axis=0) + length * jnp.sum((moments[:, 0] - mean_vec) ** 2, axis=0)
    ) / total_rows
    inv_std = lax.rsqrt(var_vec + EPS)
    normal_rows = (mixed_rows - mean_vec) * inv_std
    batch_out = normal_rows * gain_rows[5] + gain_rows[6]
    activated = jax.nn.silu(batch_out).astype(BF16)
    residual_3 = residual_2 + matmul(activated, w_cout)

    residual_4, second_ff = mlp_forward(residual_3, 1, gain_rows[3])
    block_out = layer_norm(residual_4, gain_rows[4])

    upstream, final_gain = norm_back(residual_4, gain_rows[4], out_grad)
    upstream, second_terms, second_gain = mlp_backward(
        residual_3, upstream, second_ff, 1, gain_rows[3]
    )
    second_sum = scatter(jnp.concatenate(second_terms, axis=1))

    branch_grad = upstream.astype(BF16)
    act_grad = outer_cols(branch_grad, w_cout)
    cout_terms = inner_rows(activated, branch_grad).astype(BF16).reshape(count, piece, width)
    batch_grad = act_grad * silu_slope(batch_out)
    shift_part = jnp.sum(batch_grad, axis=0)
    scale_part = jnp.sum(batch_grad * normal_rows, axis=0)
    totals = jnp.sum(gather(jnp.stack([scale_part, shift_part])), axis=0)
    mixed_grad = (
        gain_rows[5]
        * inv_std
        * (batch_grad - totals[1] / total_rows - normal_rows * (totals[0] / total_rows))
    )
    mixed_pad = jnp.pad(mixed_grad, conv_pad)
    glu_grad = depthwise(mixed_pad, taps_back)[:length]
    depth_grad = depthwise_taps(glu, pad_rows(mixed_grad))[:tap_count]
    pair_grad = jnp.concatenate(
        [glu_grad * gate, glu_grad * value_part * gate * (1.0 - gate)], axis=1
    ).astype(BF16)
    cin_terms = (
        inner_rows(pair_grad, conv_normed)
        .astype(BF16)
        .reshape(2, count, piece, width)
        .transpose(1, 0, 2, 3)
        .reshape(count, 2 * piece, width)
    )
    residual_grad, conv_gain = norm_back(residual_2, gain_rows[2], matmul(pair_grad, w_cin_t))
    upstream = upstream + residual_grad

    branch_grad = upstream.astype(BF16)
    attn_grad = pad_rows(matmul(branch_grad, w_aout_t).astype(BF16))
    aout_terms = inner_rows(branch_grad, attended)
    query_grad, key_grad, value_grad, pos_grad, bias_sums = attend_backward(
        query_a, query_b, key_rows, value_rows, pos_keys, probs, attn_grad
    )
    pack_grad = jnp.concatenate([query_grad, key_grad, value_grad], axis=1)[:length]
    qkv_terms = inner_rows(att_normed, pack_grad)
    pos_terms = inner_rows(pos_table, pos_grad)

    def square_terms(array):
        shaped = array.astype(BF16).reshape(dp, in_rows, tp, half).transpose(0, 2, 1, 3)
        return shaped.reshape(count, in_rows, half)

    qkv_terms = (
        qkv_terms.astype(BF16)
        .reshape(dp, in_rows, 3, tp, half)
        .transpose(0, 3, 1, 2, 4)
        .reshape(count, 3 * in_rows, half)
    )
    att_terms = jnp.concatenate(
        [qkv_terms, square_terms(pos_terms), square_terms(aout_terms)], axis=1
    ).reshape(count, -1, width)
    residual_grad, attend_gain = norm_back(
        residual_1, gain_rows[1], outer_cols(pack_grad, w_qkv)
    )
    upstream = upstream + residual_grad

    tokens_grad, first_terms, first_gain = mlp_backward(
        residual_0, upstream, first_ff, 0, gain_rows[0]
    )

    gain_terms = jnp.stack(
        [first_gain, attend_gain, conv_gain, second_gain, final_gain, scale_part, shift_part]
    )
    bias_terms = jnp.concatenate(
        [bias_sums[0].reshape(heads, DH), bias_sums[1].reshape(heads, DH)], axis=1
    )
    small_terms = jnp.concatenate(
        [
            gain_terms.reshape(7, count, piece).transpose(1, 0, 2).reshape(count, -1),
            depth_grad.reshape(tap_count, count, piece).transpose(1, 0, 2).reshape(count, -1),
            bias_terms.reshape(tp, bias_heads, dp, bias_width)
            .transpose(2, 0, 1, 3)
            .reshape(count, -1),
        ],
        axis=1,
    )
    small_size = small_terms.shape[1]
    small_rows = -(-small_size // width)
    small_terms = jnp.pad(small_terms, ((0, 0), (0, small_rows * width - small_size)))
    small_terms = small_terms.astype(BF16).reshape(count, small_rows, width)
    late_terms, second_sum = lax.optimization_barrier(
        (
            jnp.concatenate(
                first_terms + [att_terms, cin_terms, cout_terms, small_terms], axis=1
            ),
            second_sum,
        )
    )
    late_sum = scatter(late_terms)
    conv_start = 2 * units + att_terms.shape[1]
    small_start = conv_start + 3 * piece
    first_sum = late_sum[: 2 * units]
    att_sum = late_sum[2 * units : conv_start].reshape(-1, half)
    conv_sum = late_sum[conv_start:small_start]
    small_sum = late_sum[small_start:].astype(F32).reshape(-1)[:small_size]

    first_sum, second_sum = first_sum.astype(F32), second_sum.astype(F32)
    conv_sum, att_sum = conv_sum.astype(F32), att_sum.astype(F32)
    return (
        block_out,
        tokens_grad,
        jnp.stack([first_sum[:units].T, second_sum[:units].T])[None],
        jnp.stack([first_sum[units:], second_sum[units:]])[None],
        att_sum[: 3 * in_rows].reshape(1, in_rows, 3, half),
        att_sum[3 * in_rows : 4 * in_rows][None],
        small_sum[depth_end:].reshape(1, bias_heads, bias_width),
        att_sum[4 * in_rows :].T[None],
        conv_sum[: 2 * piece].reshape(2, piece, width).transpose(2, 0, 1)[None],
        small_sum[gain_end:depth_end].reshape(1, tap_count, piece),
        conv_sum[2 * piece :][None],
        small_sum[:gain_end].reshape(1, 7, piece),
    )


def solution(mesh):
    placed = (
        P(AXES, None),
        P(None, None, None, AXES),
        P(None, None, AXES, None),
        P(None, "dp", None, "tensor"),
        P(None, "dp", "tensor"),
        P(None, "tensor", "dp"),
        P(None, "tensor", "dp"),
        P(None, None, None, AXES),
        P(None, None, AXES),
        P(None, AXES, None),
        P(None, None, AXES),
        P(AXES, None),
    )
    return jax.shard_map(
        local,
        mesh=mesh,
        in_specs=placed,
        out_specs=(P(AXES, None),) + placed[:11],
        check_vma=False,
    )
```
